32 devices in a mesh: groups: 2 (over y), blk: 8 (over z, core), width: 2 (over x).
Axes of the slice: x: 2, y: 2, z: 4, core: 2. Of those that a mesh axis runs over, the one named last changes fastest.
Arguments:
- tokens: bfloat16 [448, 4096], P(('groups', 'blk'), 'width'), parts along dimension 0, may hold values from -6 to 6
- grad_hidden: bfloat16 [448, 28672], P('groups', 'blk'), parts along dimension 0, may hold values from -2 to 2
- codes: bfloat16 [2, 4096, 28672], P(None, 'width', 'blk'), may hold values from -8 to 7, as said below
- scales: float32 [2, 32, 28672], P(None, 'width', 'blk'), may hold values from 0.0015625 to 0.015625
- pattern: int32 [224, 32], P('blk', 'width'), may hold values from 0 to 1, as said below
Outputs:
- grad_tokens: bfloat16 [448, 4096], P(('groups', 'blk'), 'width'), parts along dimension 0
- grad_log_scales: float32 [2, 64, 28672], P(None, ('groups', 'width'), 'blk'), parts along dimension 1
The draws below stay inside these ranges and needn't reach their ends.
There are 2 independent parts, one for each index of `groups`. The reference program is written for one: setup_inputs(seed, part) draws one part's arguments, and reference() takes and returns one part's arrays. A program takes and returns all parts, laid end to end along the dimension named above; an argument that names none is the same for every part. Nothing has to cross between parts.
Inputs may be any that keep to these rules, and one draw needn't show every extreme that they name: The pattern is cut into tiles of D // (128 * 2) input blocks by 28672 // (128 * 8) hidden blocks, one for each device; every tile holds between 112 and 336 nonzero entries, and some tile holds exactly 336. `codes`: every code is a whole number.
All inputs are finite; a program needn't handle non-finite values.
Results may differ from the reference program's by a relative error of at most 0.017.
Values may be sent and summed in bfloat16 or wider, within the bound.
A program may use at most 192 MiB of HBM per device.

```python
import math
import jax
import jax.numpy as jnp
from jax import lax

D = 4096
FF = 28672
BLOCK = 128
TOKENS = 224
N_BLK = 8
N_WIDTH = 2


def draw_codes(key, part):
    whole = jax.random.randint(jax.random.fold_in(key, 21), (2, D, FF), -8, 8)
    return whole.astype(jnp.float32).astype(jnp.bfloat16)


def draw_pattern(key, part):
    rows_tile = D // (BLOCK * N_WIDTH)
    cols_tile = FF // (BLOCK * N_BLK)
    tiles = N_BLK * N_WIDTH
    per_tile = rows_tile * cols_tile
    most = per_tile * 3 // 4
    key_count = jax.random.fold_in(key, 11)
    key_full = jax.random.fold_in(key, 12)
    key_place = jax.random.fold_in(key, 13)
    counts = jax.random.randint(key_count, (tiles,), most // 3, most + 1)
    fullest = jax.random.randint(key_full, (), 0, tiles)
    counts = jnp.where(jnp.arange(tiles) == fullest, most, counts)
    keys = jax.random.split(key_place, tiles)
    ranks = jax.vmap(lambda single: jax.random.permutation(single, per_tile))(keys)
    ones = (ranks < counts[:, None]).astype(jnp.int32)
    grid = ones.reshape(N_BLK, N_WIDTH, rows_tile, cols_tile)
    return grid.transpose(0, 3, 1, 2).reshape(N_BLK * cols_tile, N_WIDTH * rows_tile)


def shard_levels(rng, shape, pieces, smallest, largest):
    gain, own = 1.0, jax.random.fold_in(rng, 6)
    for axis_at, shards_of in pieces:
        steps = jnp.exp(jax.random.uniform(jax.random.fold_in(own, axis_at), (shards_of,), jnp.float32, smallest / len(pieces), largest / len(pieces)))
        gain = gain * jnp.repeat(steps, shape[axis_at] // shards_of).reshape([-1 if axis == axis_at else 1 for axis in range(len(shape))])
    return gain


def noise(rng, shape, width, limit, pieces=(), dtype=jnp.bfloat16):
    values = width * jax.random.normal(rng, shape, jnp.float32)
    if pieces:
        values = values * shard_levels(rng, shape, pieces, -0.22, 0.18)
    return jnp.clip(values, -limit, limit).astype(dtype)


def setup_inputs(seed: int = 0, part: int = 0) -> dict:
    arg_keys = jax.random.split(jax.random.key(seed), 6)
    part_keys = jax.random.split(jax.random.fold_in(arg_keys[5], part), 6)
    tokens = noise(part_keys[0], (TOKENS, D), 1.0, 6.0, ((0, 8), (1, 2)))
    grad_hidden = noise(part_keys[1], (TOKENS, FF), 0.3, 2.0, ((1, 8),))
    codes = draw_codes(jax.random.fold_in(arg_keys[5], 71), part)
    scales = jnp.clip(jnp.exp(math.log(0.015625) - 2.3025851 * jax.random.uniform(arg_keys[3], (2, D // BLOCK, FF), jnp.float32) ** shard_levels(arg_keys[3], (2, D // BLOCK, FF), ((1, 2), (2, 8)), -0.2, 0.2)), 0.0015625, 0.015625)
    pattern = draw_pattern(jax.random.fold_in(arg_keys[5], 71), part)
    return {"tokens": tokens, "grad_hidden": grad_hidden, "codes": codes, "scales": scales, "pattern": pattern}


def rounded(value):
    return lax.optimization_barrier(value.astype(jnp.bfloat16)).astype(jnp.float32)


def reference(tokens, grad_hidden, codes, scales, pattern):
    slice_d = D // N_WIDTH
    slice_f = FF // N_BLK
    nblocks = slice_f // BLOCK
    mask_all = pattern.T.astype(jnp.float32)
    grad_total = jnp.zeros((tokens.shape[0], D), jnp.float32)
    outputs = []
    for column in range(N_BLK):
        lo = column * slice_f
        mask = jnp.repeat(mask_all[:, column * nblocks:(column + 1) * nblocks], BLOCK, axis=1)
        factor = scales[:, :, lo:lo + slice_f] * mask[None]
        values = codes[:, :, lo:lo + slice_f].astype(jnp.float32).reshape(2, D // BLOCK, BLOCK, slice_f) * factor[:, :, None, :]
        weight = values.reshape(2, D, slice_f).astype(jnp.bfloat16)
        joined = jnp.concatenate((weight[0], weight[1]), axis=1)
        hidden = jnp.zeros((tokens.shape[0], 2 * slice_f), jnp.float32)
        for piece in range(N_WIDTH):
            part = jnp.dot(tokens[:, piece * slice_d:(piece + 1) * slice_d], joined[piece * slice_d:(piece + 1) * slice_d], preferred_element_type=jnp.float32)
            hidden = hidden + rounded(part)
        gate = hidden[:, :slice_f]
        up = hidden[:, slice_f:]
        upstream = grad_hidden[:, lo:lo + slice_f].astype(jnp.float32)
        sig = jax.nn.sigmoid(gate)
        grad_gate = upstream * up * sig * (1.0 + gate * (1.0 - sig))
        grad_up = upstream * gate * sig
        grads = jnp.concatenate((grad_gate, grad_up), axis=1).astype(jnp.bfloat16)
        term = lax.dot_general(grads, joined, (((1,), (1,)), ((), ())), preferred_element_type=jnp.float32)
        grad_total = grad_total + rounded(term)
        weight_grad = lax.dot_general(tokens, grads, (((0,), (0,)), ((), ())), preferred_element_type=jnp.float32)
        codes_joined = jnp.concatenate((codes[0, :, lo:lo + slice_f], codes[1, :, lo:lo + slice_f]), axis=1).astype(jnp.float32)
        summed = (weight_grad * codes_joined).reshape(D // BLOCK, BLOCK, 2 * slice_f).sum(axis=1)
        factor_joined = jnp.concatenate((factor[0], factor[1]), axis=1)
        result = (summed * factor_joined).reshape(D // BLOCK, 2, slice_f).transpose(1, 0, 2)
        outputs.append(result)
    return grad_total.astype(jnp.bfloat16), jnp.concatenate(outputs, axis=2)
```

```python
import jax
import jax.numpy as jnp
from jax import lax
from jax.sharding import PartitionSpec as P

CHUNK_BLOCKS = 4


def on_device(width, tokens, grad_hidden, codes, scales, pattern):
    cols_tile, rows_tile = pattern.shape
    depth = codes.shape[1]
    block = depth // rows_tile
    slice_f = codes.shape[2]
    gathered = lax.all_gather(tokens, "blk", axis=0, tiled=True)
    mask = jnp.repeat(pattern.T, slice_f // cols_tile, axis=1).astype(jnp.float32)
    factor = scales * mask[None]
    step = CHUNK_BLOCKS * (slice_f // cols_tile)
    starts = list(range(0, slice_f, step))
    weights, hiddens = [], []
    for lo in starts:
        hi = min(lo + step, slice_f)
        values = codes[:, :, lo:hi].astype(jnp.float32).reshape(2, rows_tile, block, hi - lo)
        values = (values * factor[:, :, None, lo:hi]).reshape(2, depth, hi - lo).astype(jnp.bfloat16)
        parts = [
            jnp.dot(gathered, values[m], preferred_element_type=jnp.float32).astype(jnp.bfloat16)
            for m in range(2)
        ]
        mine = jnp.stack(parts)
        if width == 2:
            other = lax.ppermute(mine, "width", [(0, 1), (1, 0)])
            hidden = mine.astype(jnp.float32) + other.astype(jnp.float32)
        else:
            hidden = lax.psum(mine, "width").astype(jnp.float32)
        weights.append(values)
        hiddens.append(hidden)
    total = 0.0
    results = []
    for i, lo in enumerate(starts):
        hi = min(lo + step, slice_f)
        gate, up = hiddens[i][0], hiddens[i][1]
        grad_in = grad_hidden[:, lo:hi].astype(jnp.float32)
        sig = jax.nn.sigmoid(gate)
        grads = [
            (grad_in * up * sig * (1.0 + gate * (1.0 - sig))).astype(jnp.bfloat16),
            (grad_in * gate * sig).astype(jnp.bfloat16),
        ]
        sums = []
        for m in range(2):
            total = total + lax.dot_general(
                grads[m], weights[i][m], (((1,), (1,)), ((), ())), preferred_element_type=jnp.float32
            )
            weight_grad = lax.dot_general(
                gathered, grads[m], (((0,), (0,)), ((), ())), preferred_element_type=jnp.float32
            )
            sums.append(
                (weight_grad * codes[m, :, lo:hi].astype(jnp.float32))
                .reshape(rows_tile, block, hi - lo)
                .sum(axis=1)
            )
        results.append(jnp.stack(sums) * factor[:, :, lo:hi])
    grad_tokens = lax.psum_scatter(
        total.astype(jnp.bfloat16), "blk", scatter_dimension=0, tiled=True
    )
    return grad_tokens, jnp.concatenate(results, axis=2)


def solution(mesh):
    width = mesh.shape["width"]

    def body(*args):
        return on_device(width, *args)

    return jax.shard_map(
        body,
        mesh=mesh,
        in_specs=(
            P(("groups", "blk"), "width"),
            P("groups", "blk"),
            P(None, "width", "blk"),
            P(None, "width", "blk"),
            P("blk", "width"),
        ),
        out_specs=(P(("groups", "blk"), "width"), P(None, ("groups", "width"), "blk")),
        check_vma=False,
    )
```

```python
import jax
import jax.numpy as jnp
from jax import lax
from jax.experimental import pallas as pl
from jax.experimental.pallas import tpu as pltpu
from jax.sharding import PartitionSpec as P


def dequantize(codes, scales, pattern):
    rows_tile = scales.shape[1]
    block = codes.shape[1] // rows_tile
    cols = codes.shape[2]
    mask = jnp.repeat(pattern.T, block, axis=1).astype(jnp.float32)
    factor = scales * mask[None]
    values = codes.astype(jnp.float32).reshape(2, rows_tile, block, cols) * factor[:, :, None, :]
    weight = values.reshape(codes.shape).astype(jnp.bfloat16)
    return (jnp.concatenate((weight[0], weight[1]), axis=1), factor)


def back_gates(hidden, upstream):
    half = upstream.shape[1]
    gate = hidden[:, :half]
    up = hidden[:, half:]
    grad_in = upstream.astype(jnp.float32)
    sig = jax.nn.sigmoid(gate)
    grad_gate = grad_in * up * sig * (1.0 + gate * (1.0 - sig))
    grad_up = grad_in * gate * sig
    return jnp.concatenate((grad_gate, grad_up), axis=1).astype(jnp.bfloat16)


def on_device(tokens, grad_hidden, codes, scales, pattern):
    cols_tile, rows_tile = pattern.shape
    block = codes.shape[1] // rows_tile
    slice_f = codes.shape[2]
    gathered = lax.all_gather(tokens, "blk", axis=0, tiled=True)
    joined, factor = dequantize(codes, scales, pattern)
    hidden = lax.psum(
        jnp.dot(gathered, joined, preferred_element_type=jnp.float32).astype(jnp.bfloat16), "width"
    ).astype(jnp.float32)
    grads = back_gates(hidden, grad_hidden)
    grad_tokens = lax.psum_scatter(
        lax.dot_general(
            grads, joined, (((1,), (1,)), ((), ())), preferred_element_type=jnp.float32
        ).astype(jnp.bfloat16),
        "blk",
        scatter_dimension=0,
        tiled=True,
    )
    weight_grad = lax.dot_general(
        gathered, grads, (((0,), (0,)), ((), ())), preferred_element_type=jnp.float32
    )
    codes_joined = jnp.concatenate((codes[0], codes[1]), axis=1).astype(jnp.float32)
    summed = (weight_grad * codes_joined).reshape(rows_tile, block, 2 * slice_f).sum(axis=1)
    factor_joined = jnp.concatenate((factor[0], factor[1]), axis=1)
    return (grad_tokens, (summed * factor_joined).reshape(rows_tile, 2, slice_f).transpose(1, 0, 2))


FC = 256
AHEAD = 4
FIRST = 6
PAD = 32


def dot(a, b, dims=((1,), (0,))):
    return lax.dot_general(a, b, (dims, ((), ())), preferred_element_type=jnp.float32)


def kernel(
    tokens_ref, hidden_ref, codes_ref, scales_ref, pattern_ref, out_ref, gls_ref,
    w_ref, mine_ref, theirs_ref, gath_ref, tok_ref, tokt_ref, gh_ref, acc_ref,
    far_out, sib_in, far_sum, far_in, near_out, near_in,
    codes_sem, gh_sem, xs_sem, xr_sem, ags_sem, agr_sem, sibs_sem, sibr_sem,
    fars_sem, farr_sem, nears_sem, nearr_sem,
):
    chunks, _, depth, _ = w_ref.shape
    items = 2 * chunks
    rows = tok_ref.shape[1]
    own_rows = tokens_ref.shape[0]
    groups = scales_ref.shape[1]
    block = depth // groups
    blk = lax.axis_index("blk")
    wide = lax.axis_index("width")
    half = blk // 4
    place = lax.rem(blk, 4)
    core = lax.rem(blk, 2)
    zlow = place // 2

    def peer(rel):
        bit0 = core if rel % 2 == 0 else 1 - core
        bit1 = zlow if (rel // 2) % 2 == 0 else 1 - zlow
        bit2 = half if rel // 4 == 0 else 1 - half
        return bit2 * 4 + bit1 * 2 + bit0

    def remote(src, dst, send, recv, target):
        return pltpu.make_async_remote_copy(
            src_ref=src, dst_ref=dst, send_sem=send, recv_sem=recv,
            device_id=target, device_id_type=pl.DeviceIdType.MESH,
        )

    def codes_copy(c):
        return pltpu.make_async_copy(
            codes_ref.at[:, :, pl.ds(pl.multiple_of(c * FC, FC), FC)], w_ref.at[c], codes_sem.at[c]
        )

    def gh_copy(g):
        which = half if g == 0 else 1 - half
        return pltpu.make_async_copy(
            hidden_ref.at[pl.ds(pl.multiple_of(which * rows, 16), rows)], gh_ref.at[g], gh_sem.at[g]
        )

    def ag_copy(rel):
        if rel in (1, 2, 4, 6):
            return remote(gath_ref.at[0], gath_ref.at[rel], ags_sem.at[rel], agr_sem.at[rel], {"blk": peer(rel)})
        return remote(gath_ref.at[rel - 1], gath_ref.at[rel], ags_sem.at[rel], agr_sem.at[rel], {"blk": peer(1)})

    def x_copy(i):
        return remote(mine_ref.at[i], theirs_ref.at[i], xs_sem.at[i], xr_sem.at[i], {"width": 1 - wide})

    def sib_copy(z):
        return remote(far_out.at[2 * z + 1 - core], sib_in.at[z], sibs_sem.at[z], sibr_sem.at[z], {"blk": peer(1)})

    def far_copy(z):
        target = (1 - half) * 4 + z * 2 + core
        return remote(far_sum.at[z], far_in.at[zlow], fars_sem.at[z], farr_sem.at[zlow], {"blk": target})

    def near_copy(rel):
        j = lax.rem(peer(rel), 4)
        return remote(near_out.at[j], near_in.at[rel - 1], nears_sem.at[rel - 1], nearr_sem.at[rel - 1], {"blk": peer(rel)})

    lax.fori_loop(0, chunks, lambda c, _: (codes_copy(c).start(), 0)[1], 0)
    for g in range(2):
        gh_copy(g).start()

    barrier = pltpu.get_barrier_semaphore()
    pl.semaphore_signal(barrier, inc=1, device_id={"width": 1 - wide}, device_id_type=pl.DeviceIdType.MESH)
    for rel in (1, 2, 3, 4, 6):
        pl.semaphore_signal(barrier, inc=1, device_id={"blk": peer(rel)}, device_id_type=pl.DeviceIdType.MESH)
    gath_ref[0] = jnp.concatenate(
        [tokens_ref[...], jnp.zeros((PAD - own_rows, depth), tokens_ref.dtype)], axis=0
    )
    acc_ref[...] = jnp.zeros_like(acc_ref)
    pl.semaphore_wait(barrier, 6)
    for rel in (2, 1, 6, 4):
        ag_copy(rel).start()

    def select(shape, dim):
        short = lax.broadcasted_iota(jnp.int32, shape, dim)
        long = lax.broadcasted_iota(jnp.int32, shape, 1 - dim)
        slot = long >> 5
        hit = (long - 4 * slot == short) & (long - 32 * slot < own_rows)
        return jnp.where(hit, 1.0, 0.0).astype(jnp.bfloat16)

    def compact(g):
        pick = select((rows, 4 * PAD), 0)
        joined = []
        for j in range(4):
            jz, jc = j // 2, j % 2
            dz = jnp.where(zlow == jz, 0, 1)
            dc = jnp.where(core == jc, 0, 1)
            joined.append(gath_ref[4 * g + 2 * dz + dc])
        tok_ref[g] = dot(pick, jnp.concatenate(joined, axis=0)).astype(jnp.bfloat16)

    def spread(g):
        pick = select((4 * PAD, rows), 1)
        return dot(pick, acc_ref[g].astype(jnp.bfloat16)).astype(jnp.bfloat16).reshape(4, PAD, depth)

    ag_copy(2).wait_recv()
    ag_copy(3).start()
    ag_copy(1).wait_recv()
    ag_copy(3).wait_recv()
    compact(0)
    for g in range(2):
        gh_copy(g).wait()

    def place_of(i):
        first = i < FIRST
        other = (i >= FIRST) & (i < FIRST + chunks)
        g = jnp.where(other, 1, 0)
        c = jnp.where(first, i, jnp.where(other, i - FIRST, i - chunks))
        return g, c

    def prepare(c):
        codes_copy(c).wait()
        cols = pl.ds(pl.multiple_of(c * FC, FC), FC)
        lane = lax.broadcasted_iota(jnp.int32, (1, FC), 1)

        def body(r, _):
            left = pattern_ref[2 * c, r].astype(jnp.float32)
            right = pattern_ref[2 * c + 1, r].astype(jnp.float32)
            kept = jnp.where(lane < block, left, right)
            rowsel = pl.ds(pl.multiple_of(r * block, block), block)
            for m in range(2):
                factor = scales_ref[m, pl.ds(r, 1), cols] * kept
                w_ref[c, m, rowsel, :] = (
                    w_ref[c, m, rowsel, :].astype(jnp.float32) * factor
                ).astype(jnp.bfloat16)
            return 0

        lax.fori_loop(0, groups, body, 0)

    def forward(i):
        g, c = place_of(i)
        pl.when((i < FIRST) | ((g == 1) & (c >= FIRST)))(lambda: prepare(c))
        for m in range(2):
            mine_ref[i, m] = dot(tok_ref[g], w_ref[c, m]).astype(jnp.bfloat16)
        x_copy(i).start()

    def backward(i):
        g, c = place_of(i)
        x_copy(i).wait_recv()
        cols = pl.ds(pl.multiple_of(c * FC, FC), FC)
        gate = mine_ref[i, 0].astype(jnp.float32) + theirs_ref[i, 0].astype(jnp.float32)
        up = mine_ref[i, 1].astype(jnp.float32) + theirs_ref[i, 1].astype(jnp.float32)
        grad_in = gh_ref[g, :, cols].astype(jnp.float32)
        sig = jax.nn.sigmoid(gate)
        theirs_ref[i, 0] = (grad_in * up * sig * (1.0 + gate * (1.0 - sig))).astype(jnp.bfloat16)
        theirs_ref[i, 1] = (grad_in * gate * sig).astype(jnp.bfloat16)
        both = dot(theirs_ref[i, 0], w_ref[c, 0], ((1,), (1,)))
        acc_ref[g] += both + dot(theirs_ref[i, 1], w_ref[c, 1], ((1,), (1,)))

        @pl.when((i >= FIRST) & (i < 2 * FIRST) | (i >= FIRST + chunks))
        def _():
            own = jnp.where(i < 2 * FIRST, i - FIRST, i)
            far = jnp.where(i < 2 * FIRST, i, i - chunks + FIRST)
            for m in range(2):
                grads = jnp.concatenate([theirs_ref[own, m], theirs_ref[far, m]], axis=0)
                for q in range(4):
                    part = depth // 4
                    wg = dot(tokt_ref[q * part : (q + 1) * part, :], grads)
                    prod = wg * w_ref[c, m, q * part : (q + 1) * part, :].astype(jnp.float32)
                    gls_ref[m, q * (groups // 4) : (q + 1) * (groups // 4), cols] = (
                        prod.reshape(groups // 4, block, FC).sum(axis=1)
                    )

    def second_half():
        for rel in (5, 7):
            ag_copy(rel).wait_recv()
        compact(1)
        eye_r = lax.broadcasted_iota(jnp.int32, (FC, FC), 0)
        eye_c = lax.broadcasted_iota(jnp.int32, (FC, FC), 1)
        eye = jnp.where(eye_r == eye_c, 1.0, 0.0).astype(jnp.bfloat16)
        for q in range(depth // FC):
            sub = slice(q * FC, (q + 1) * FC)
            whole = jnp.concatenate([tok_ref[0, :, sub], tok_ref[1, :, sub]], axis=0)
            tokt_ref[sub, :] = dot(eye, whole, ((1,), (1,))).astype(jnp.bfloat16)

    def hand_on():
        for rel in (4, 6):
            ag_copy(rel).wait_recv()
            ag_copy(rel + 1).start()

    def far_start():
        far_out[...] = spread(1)
        for z in range(2):
            sib_copy(z).start()

    def far_finish():
        for z in range(2):
            sib_copy(z).wait_recv()
            far_sum[z] = (
                far_out[2 * z + core].astype(jnp.float32) + sib_in[z].astype(jnp.float32)
            ).astype(jnp.bfloat16)
            far_copy(z).start()

    def step(s, _):
        pl.when(s == FIRST - 2)(hand_on)
        pl.when(s == FIRST)(second_half)
        pl.when(s < items)(lambda: forward(s))
        pl.when(s >= AHEAD)(lambda: backward(s - AHEAD))
        pl.when(s == FIRST + chunks + AHEAD - 1)(far_start)
        pl.when(s == FIRST + chunks + AHEAD)(far_finish)
        return 0

    lax.fori_loop(0, items + AHEAD, step, 0)
    near_out[...] = spread(0)
    for rel in (3, 2, 1):
        near_copy(rel).start()
    total = near_out[place].astype(jnp.float32)
    for z in range(2):
        remote(far_sum.at[z], far_in.at[z], fars_sem.at[z], farr_sem.at[z], {"blk": peer(4)}).wait_recv()
        total = total + far_in[z].astype(jnp.float32)
    for rel in (1, 2, 3):
        near_copy(rel).wait_recv()
        total = total + near_in[rel - 1].astype(jnp.float32)
    out_ref[...] = total[:own_rows].astype(out_ref.dtype)

    for rel in (1, 2, 3, 4, 5, 6, 7):
        ag_copy(rel).wait_send()
    lax.fori_loop(0, items, lambda i, _: (x_copy(i).wait_send(), 0)[1], 0)
    for z in range(2):
        sib_copy(z).wait_send()
        far_copy(z).wait_send()
    for rel in (1, 2, 3):
        near_copy(rel).wait_send()


def fused(tokens, grad_hidden, codes, scales, pattern):
    own_rows, depth = tokens.shape
    slice_f = codes.shape[2]
    chunks = slice_f // FC
    items = 2 * chunks
    rows = 4 * own_rows
    bf16 = jnp.bfloat16
    vmem = pl.BlockSpec(memory_space=pltpu.VMEM)
    hbm = pl.BlockSpec(memory_space=pl.ANY)
    dma = pltpu.SemaphoreType.DMA
    return pl.pallas_call(
        kernel,
        out_shape=(
            jax.ShapeDtypeStruct((own_rows, depth), bf16),
            jax.ShapeDtypeStruct(scales.shape, jnp.float32),
        ),
        in_specs=[vmem, hbm, hbm, vmem, pl.BlockSpec(memory_space=pltpu.SMEM)],
        out_specs=(vmem, vmem),
        scratch_shapes=[
            pltpu.VMEM((chunks, 2, depth, FC), bf16),
            pltpu.VMEM((items, 2, rows, FC), bf16),
            pltpu.VMEM((items, 2, rows, FC), bf16),
            pltpu.VMEM((8, PAD, depth), bf16),
            pltpu.VMEM((2, rows, depth), bf16),
            pltpu.VMEM((depth, 2 * rows), bf16),
            pltpu.VMEM((2, rows, slice_f), bf16),
            pltpu.VMEM((2, rows, depth), jnp.float32),
            pltpu.VMEM((4, PAD, depth), bf16),
            pltpu.VMEM((2, PAD, depth), bf16),
            pltpu.VMEM((2, PAD, depth), bf16),
            pltpu.VMEM((2, PAD, depth), bf16),
            pltpu.VMEM((4, PAD, depth), bf16),
            pltpu.VMEM((3, PAD, depth), bf16),
            dma((chunks,)), dma((2,)), dma((items,)), dma((items,)), dma((8,)), dma((8,)),
            dma((2,)), dma((2,)), dma((2,)), dma((2,)), dma((3,)), dma((3,)),
        ],
        compiler_params=pltpu.CompilerParams(
            collective_id=0, has_side_effects=True, vmem_limit_bytes=60 * 1024 * 1024
        ),
        cost_estimate=pl.CostEstimate(
            flops=6 * 2 * own_rows * 8 * depth * 2 * slice_f // 2,
            bytes_accessed=codes.size * 2, transcendentals=0,
        ),
    )(tokens, grad_hidden, codes, scales, pattern)


def device_program(mesh):
    def run(tokens, grad_hidden, codes, scales, pattern):
        fits = (
            mesh.shape["blk"] == 8
            and mesh.shape["width"] == 2
            and tokens.shape[0] == 28
            and codes.shape[1:] == (2048, 3584)
        )
        call = fused if fits else on_device
        return call(tokens, grad_hidden, codes, scales, pattern)

    return run


def solution(mesh):
    return jax.shard_map(
        device_program(mesh),
        mesh=mesh,
        in_specs=(
            P(("groups", "blk"), "width"),
            P("groups", "blk"),
            P(None, "width", "blk"),
            P(None, "width", "blk"),
            P("blk", "width"),
        ),
        out_specs=(P(("groups", "blk"), "width"), P(None, ("groups", "width"), "blk")),
        check_vma=False,
    )
```

```python
import jax
import jax.numpy as jnp
from jax import lax
from jax.experimental import pallas as pl
from jax.experimental.pallas import tpu as pltpu
from jax.sharding import PartitionSpec as P


def dequantize(codes, scales, pattern):
    rows_tile = scales.shape[1]
    block = codes.shape[1] // rows_tile
    cols = codes.shape[2]
    mask = jnp.repeat(pattern.T, block, axis=1).astype(jnp.float32)
    factor = scales * mask[None]
    values = codes.astype(jnp.float32).reshape(2, rows_tile, block, cols) * factor[:, :, None, :]
    weight = values.reshape(codes.shape).astype(jnp.bfloat16)
    return (jnp.concatenate((weight[0], weight[1]), axis=1), factor)


def back_gates(hidden, upstream):
    half = upstream.shape[1]
    gate = hidden[:, :half]
    up = hidden[:, half:]
    grad_in = upstream.astype(jnp.float32)
    sig = jax.nn.sigmoid(gate)
    grad_gate = grad_in * up * sig * (1.0 + gate * (1.0 - sig))
    grad_up = grad_in * gate * sig
    return jnp.concatenate((grad_gate, grad_up), axis=1).astype(jnp.bfloat16)


def on_device(tokens, grad_hidden, codes, scales, pattern):
    cols_tile, rows_tile = pattern.shape
    block = codes.shape[1] // rows_tile
    slice_f = codes.shape[2]
    gathered = lax.all_gather(tokens, "blk", axis=0, tiled=True)
    joined, factor = dequantize(codes, scales, pattern)
    hidden = lax.psum(
        jnp.dot(gathered, joined, preferred_element_type=jnp.float32).astype(jnp.bfloat16), "width"
    ).astype(jnp.float32)
    grads = back_gates(hidden, grad_hidden)
    grad_tokens = lax.psum_scatter(
        lax.dot_general(
            grads, joined, (((1,), (1,)), ((), ())), preferred_element_type=jnp.float32
        ).astype(jnp.bfloat16),
        "blk",
        scatter_dimension=0,
        tiled=True,
    )
    weight_grad = lax.dot_general(
        gathered, grads, (((0,), (0,)), ((), ())), preferred_element_type=jnp.float32
    )
    codes_joined = jnp.concatenate((codes[0], codes[1]), axis=1).astype(jnp.float32)
    summed = (weight_grad * codes_joined).reshape(rows_tile, block, 2 * slice_f).sum(axis=1)
    factor_joined = jnp.concatenate((factor[0], factor[1]), axis=1)
    return (grad_tokens, (summed * factor_joined).reshape(rows_tile, 2, slice_f).transpose(1, 0, 2))


FC = 256
AHEAD = 4
FETCH = 3
FIRST = 8
PAD = 32


def dot(a, b, dims=((1,), (0,))):
    return lax.dot_general(a, b, (dims, ((), ())), preferred_element_type=jnp.float32)


def kernel(
    tokens_ref, hidden_ref, codes_ref, scales_ref, pattern_ref, out_ref, gls_ref,
    w_ref, mine_ref, theirs_ref, gath_ref, tok_ref, tokt_ref, gh_ref, acc_ref,
    far_out, sib_in, far_sum, far_in, near_out, near_in, factor_ref,
    codes_sem, gh_sem, xs_sem, xr_sem, ags_sem, agr_sem, sibs_sem, sibr_sem,
    fars_sem, farr_sem, nears_sem, nearr_sem,
):
    chunks, _, depth, _ = w_ref.shape
    items = 2 * chunks
    rows = tok_ref.shape[1]
    own_rows = tokens_ref.shape[0]
    groups = scales_ref.shape[1]
    block = depth // groups
    blk = lax.axis_index("blk")
    wide = lax.axis_index("width")
    half = blk // 4
    place = lax.rem(blk, 4)
    core = lax.rem(blk, 2)
    zlow = place // 2

    def peer(rel):
        bit0 = core if rel % 2 == 0 else 1 - core
        bit1 = zlow if (rel // 2) % 2 == 0 else 1 - zlow
        bit2 = half if rel // 4 == 0 else 1 - half
        return bit2 * 4 + bit1 * 2 + bit0

    def remote(src, dst, send, recv, target):
        return pltpu.make_async_remote_copy(
            src_ref=src, dst_ref=dst, send_sem=send, recv_sem=recv,
            device_id=target, device_id_type=pl.DeviceIdType.MESH,
        )

    def codes_copy(c):
        return pltpu.make_async_copy(
            codes_ref.at[:, :, pl.ds(pl.multiple_of(c * FC, FC), FC)], w_ref.at[c], codes_sem.at[c]
        )

    def gh_copy(g):
        which = half if g == 0 else 1 - half
        return pltpu.make_async_copy(
            hidden_ref.at[pl.ds(pl.multiple_of(which * rows, 16), rows)], gh_ref.at[g], gh_sem.at[g]
        )

    def ag_copy(rel):
        if rel in (1, 2, 4, 6):
            return remote(gath_ref.at[0], gath_ref.at[rel], ags_sem.at[rel], agr_sem.at[rel], {"blk": peer(rel)})
        return remote(gath_ref.at[rel - 1], gath_ref.at[rel], ags_sem.at[rel], agr_sem.at[rel], {"blk": peer(1)})

    def x_copy(i):
        return remote(mine_ref.at[i], theirs_ref.at[i], xs_sem.at[i], xr_sem.at[i], {"width": 1 - wide})

    def sib_copy(z):
        return remote(far_out.at[2 * z + 1 - core], sib_in.at[z], sibs_sem.at[z], sibr_sem.at[z], {"blk": peer(1)})

    def far_copy(z):
        target = (1 - half) * 4 + z * 2 + core
        return remote(far_sum.at[z], far_in.at[zlow], fars_sem.at[z], farr_sem.at[zlow], {"blk": target})

    def near_copy(rel):
        j = lax.rem(peer(rel), 4)
        return remote(near_out.at[j], near_in.at[rel - 1], nears_sem.at[rel - 1], nearr_sem.at[rel - 1], {"blk": peer(rel)})

    lax.fori_loop(0, FETCH, lambda c, _: (codes_copy(c).start(), 0)[1], 0)
    for g in range(2):
        gh_copy(g).start()

    barrier = pltpu.get_barrier_semaphore()
    pl.semaphore_signal(barrier, inc=1, device_id={"width": 1 - wide}, device_id_type=pl.DeviceIdType.MESH)
    for rel in (1, 2, 3, 4, 6):
        pl.semaphore_signal(barrier, inc=1, device_id={"blk": peer(rel)}, device_id_type=pl.DeviceIdType.MESH)
    gath_ref[0] = jnp.concatenate(
        [tokens_ref[...], jnp.zeros((PAD - own_rows, depth), tokens_ref.dtype)], axis=0
    )
    pl.semaphore_wait(barrier, 6)
    for rel in (2, 1):
        ag_copy(rel).start()

    def select(shape, dim):
        short = lax.broadcasted_iota(jnp.int32, shape, dim)
        long = lax.broadcasted_iota(jnp.int32, shape, 1 - dim)
        slot = long >> 5
        hit = (long - 4 * slot == short) & (long - 32 * slot < own_rows)
        return jnp.where(hit, 1.0, 0.0).astype(jnp.bfloat16)

    def compact(g):
        pick = select((rows, 4 * PAD), 0)
        joined = []
        for j in range(4):
            jz, jc = j // 2, j % 2
            dz = jnp.where(zlow == jz, 0, 1)
            dc = jnp.where(core == jc, 0, 1)
            joined.append(gath_ref[4 * g + 2 * dz + dc])
        tok_ref[g] = dot(pick, jnp.concatenate(joined, axis=0)).astype(jnp.bfloat16)

    def spread(g):
        pick = select((4 * PAD, rows), 1)
        return dot(pick, acc_ref[g].astype(jnp.bfloat16)).astype(jnp.bfloat16).reshape(4, PAD, depth)

    acc_ref[...] = jnp.zeros_like(acc_ref)
    kept_blocks = pattern_ref[...].astype(jnp.float32).astype(jnp.bfloat16)
    column = lax.broadcasted_iota(jnp.int32, (pattern_ref.shape[0], scales_ref.shape[2]), 1)
    which = lax.broadcasted_iota(jnp.int32, column.shape, 0)
    inside = (column >= which * block) & (column < (which + 1) * block)
    mask = dot(kept_blocks, jnp.where(inside, 1.0, 0.0).astype(jnp.bfloat16), ((0,), (0,)))
    for m in range(2):
        factor_ref[m] = scales_ref[m] * mask
    ag_copy(2).wait_recv()
    ag_copy(3).start()
    for rel in (6, 4):
        ag_copy(rel).start()
    ag_copy(1).wait_recv()
    ag_copy(3).wait_recv()
    compact(0)
    for g in range(2):
        gh_copy(g).wait()

    def place_of(i):
        first = i < FIRST
        other = (i >= FIRST) & (i < FIRST + chunks)
        g = jnp.where(other, 1, 0)
        c = jnp.where(first, i, jnp.where(other, i - FIRST, i - chunks))
        return g, c

    def prepare(c):
        codes_copy(c).wait()
        pl.when(c + FETCH < chunks)(lambda: codes_copy(c + FETCH).start())
        cols = pl.ds(pl.multiple_of(c * FC, FC), FC)

        def body(r, _):
            rowsel = pl.ds(pl.multiple_of(r * block, block), block)
            for m in range(2):
                factor = factor_ref[m, pl.ds(r, 1), cols]
                w_ref[c, m, rowsel, :] = (
                    w_ref[c, m, rowsel, :].astype(jnp.float32) * factor
                ).astype(jnp.bfloat16)
            return 0

        lax.fori_loop(0, groups, body, 0)

    def forward(i):
        g, c = place_of(i)
        pl.when((i < FIRST) | ((g == 1) & (c >= FIRST)))(lambda: prepare(c))
        for m in range(2):
            mine_ref[i, m] = dot(tok_ref[g], w_ref[c, m]).astype(jnp.bfloat16)
        x_copy(i).start()

    def backward(i):
        g, c = place_of(i)
        x_copy(i).wait_recv()
        cols = pl.ds(pl.multiple_of(c * FC, FC), FC)
        gate = mine_ref[i, 0].astype(jnp.float32) + theirs_ref[i, 0].astype(jnp.float32)
        up = mine_ref[i, 1].astype(jnp.float32) + theirs_ref[i, 1].astype(jnp.float32)
        grad_in = gh_ref[g, :, cols].astype(jnp.float32)
        sig = jax.nn.sigmoid(gate)
        theirs_ref[i, 0] = (grad_in * up * sig * (1.0 + gate * (1.0 - sig))).astype(jnp.bfloat16)
        theirs_ref[i, 1] = (grad_in * gate * sig).astype(jnp.bfloat16)
        both = dot(theirs_ref[i, 0], w_ref[c, 0], ((1,), (1,)))
        acc_ref[g] += both + dot(theirs_ref[i, 1], w_ref[c, 1], ((1,), (1,)))
        complete = (i >= FIRST) & (i < 2 * FIRST) | (i >= FIRST + chunks)
        pl.when(complete & (i < items - 1))(lambda: step_grads(i))

    def step_grads(i):
        _, c = place_of(i)
        cols = pl.ds(pl.multiple_of(c * FC, FC), FC)
        own = jnp.where(i < 2 * FIRST, i - FIRST, i)
        far = jnp.where(i < 2 * FIRST, i, i - chunks + FIRST)
        for m in range(2):
            grads = jnp.concatenate([theirs_ref[own, m], theirs_ref[far, m]], axis=0)
            for q in range(4):
                part = depth // 4
                wg = dot(tokt_ref[q * part : (q + 1) * part, :], grads)
                prod = wg * w_ref[c, m, q * part : (q + 1) * part, :].astype(jnp.float32)
                gls_ref[m, q * (groups // 4) : (q + 1) * (groups // 4), cols] = (
                    prod.reshape(groups // 4, block, FC).sum(axis=1)
                )

    def second_half():
        for rel in (5, 7):
            ag_copy(rel).wait_recv()
        compact(1)
        eye_r = lax.broadcasted_iota(jnp.int32, (FC, FC), 0)
        eye_c = lax.broadcasted_iota(jnp.int32, (FC, FC), 1)
        eye = jnp.where(eye_r == eye_c, 1.0, 0.0).astype(jnp.bfloat16)
        for q in range(depth // FC):
            sub = slice(q * FC, (q + 1) * FC)
            whole = jnp.concatenate([tok_ref[0, :, sub], tok_ref[1, :, sub]], axis=0)
            tokt_ref[sub, :] = dot(eye, whole, ((1,), (1,))).astype(jnp.bfloat16)

    def hand_on():
        for rel in (4, 6):
            ag_copy(rel).wait_recv()
            ag_copy(rel + 1).start()

    def far_start():
        far_out[...] = spread(1)
        for z in range(2):
            sib_copy(z).start()

    def far_finish():
        for z in range(2):
            sib_copy(z).wait_recv()
            far_sum[z] = (
                far_out[2 * z + core].astype(jnp.float32) + sib_in[z].astype(jnp.float32)
            ).astype(jnp.bfloat16)
            far_copy(z).start()

    def step(s, _):
        pl.when(s == FIRST - 2)(hand_on)
        pl.when(s == FIRST)(second_half)
        pl.when(s < items)(lambda: forward(s))
        pl.when(s >= AHEAD)(lambda: backward(s - AHEAD))
        pl.when(s == FIRST + chunks + AHEAD - 1)(far_start)
        pl.when(s == FIRST + chunks + AHEAD)(far_finish)
        return 0

    lax.fori_loop(0, items + AHEAD, step, 0)
    near_out[...] = spread(0)
    for rel in (3, 2, 1):
        near_copy(rel).start()
    lax.fori_loop(items - 1, items, lambda i, _: (step_grads(i), 0)[1], 0)
    total = near_out[place].astype(jnp.float32)
    for z in range(2):
        remote(far_sum.at[z], far_in.at[z], fars_sem.at[z], farr_sem.at[z], {"blk": peer(4)}).wait_recv()
        total = total + far_in[z].astype(jnp.float32)
    for rel in (1, 2, 3):
        near_copy(rel).wait_recv()
        total = total + near_in[rel - 1].astype(jnp.float32)
    out_ref[...] = total[:own_rows].astype(out_ref.dtype)

    for rel in (1, 2, 3, 4, 5, 6, 7):
        ag_copy(rel).wait_send()
    lax.fori_loop(0, items, lambda i, _: (x_copy(i).wait_send(), 0)[1], 0)
    for z in range(2):
        sib_copy(z).wait_send()
        far_copy(z).wait_send()
    for rel in (1, 2, 3):
        near_copy(rel).wait_send()


def fused(tokens, grad_hidden, codes, scales, pattern):
    own_rows, depth = tokens.shape
    slice_f = codes.shape[2]
    chunks = slice_f // FC
    items = 2 * chunks
    rows = 4 * own_rows
    bf16 = jnp.bfloat16
    vmem = pl.BlockSpec(memory_space=pltpu.VMEM)
    hbm = pl.BlockSpec(memory_space=pl.ANY)
    dma = pltpu.SemaphoreType.DMA
    return pl.pallas_call(
        kernel,
        out_shape=(
            jax.ShapeDtypeStruct((own_rows, depth), bf16),
            jax.ShapeDtypeStruct(scales.shape, jnp.float32),
        ),
        in_specs=[vmem, hbm, hbm, vmem, vmem],
        out_specs=(vmem, vmem),
        scratch_shapes=[
            pltpu.VMEM((chunks, 2, depth, FC), bf16),
            pltpu.VMEM((items, 2, rows, FC), bf16),
            pltpu.VMEM((items, 2, rows, FC), bf16),
            pltpu.VMEM((8, PAD, depth), bf16),
            pltpu.VMEM((2, rows, depth), bf16),
            pltpu.VMEM((depth, 2 * rows), bf16),
            pltpu.VMEM((2, rows, slice_f), bf16),
            pltpu.VMEM((2, rows, depth), jnp.float32),
            pltpu.VMEM((4, PAD, depth), bf16),
            pltpu.VMEM((2, PAD, depth), bf16),
            pltpu.VMEM((2, PAD, depth), bf16),
            pltpu.VMEM((2, PAD, depth), bf16),
            pltpu.VMEM((4, PAD, depth), bf16),
            pltpu.VMEM((3, PAD, depth), bf16),
            pltpu.VMEM(scales.shape, jnp.float32),
            dma((chunks,)), dma((2,)), dma((items,)), dma((items,)), dma((8,)), dma((8,)),
            dma((2,)), dma((2,)), dma((2,)), dma((2,)), dma((3,)), dma((3,)),
        ],
        compiler_params=pltpu.CompilerParams(
            collective_id=0, has_side_effects=True, vmem_limit_bytes=60 * 1024 * 1024
        ),
        cost_estimate=pl.CostEstimate(
            flops=6 * 2 * own_rows * 8 * depth * 2 * slice_f // 2,
            bytes_accessed=codes.size * 2, transcendentals=0,
        ),
    )(tokens, grad_hidden, codes, scales, pattern)


def device_program(mesh):
    def run(tokens, grad_hidden, codes, scales, pattern):
        fits = (
            mesh.shape["blk"] == 8
            and mesh.shape["width"] == 2
            and tokens.shape[0] == 28
            and codes.shape[1:] == (2048, 3584)
        )
        call = fused if fits else on_device
        return call(tokens, grad_hidden, codes, scales, pattern)

    return run


def solution(mesh):
    return jax.shard_map(
        device_program(mesh),
        mesh=mesh,
        in_specs=(
            P(("groups", "blk"), "width"),
            P("groups", "blk"),
            P(None, "width", "blk"),
            P(None, "width", "blk"),
            P("blk", "width"),
        ),
        out_specs=(P(("groups", "blk"), "width"), P(None, ("groups", "width"), "blk")),
        check_vma=False,
    )
```
